128 devices in a mesh: box: 8 (over y, core), ctr: 16 (over z, x).
Axes of the slice: x: 4, y: 4, z: 4, core: 2. Of those that a mesh axis runs over, the one named last changes fastest.
Arguments:
- box_locals: bfloat16 [289, 16384], P(None, 'box'), may hold values from -6 to 6
- centre_box: int32 [262144], P(('box', 'ctr')), may hold values from 0 to 16383, as said below
- centre_rho: float32 [262144], P(('box', 'ctr')), may hold values from 0.85 to 1
- panel_sources: bfloat16 [131072, 128], P('ctr'), may hold values from -6 to 6
- centre_near: int32 [8, 262144], P(None, ('box', 'ctr')), may hold values from 0 to 131071, as said below
- near_count: int32 [262144], P(('box', 'ctr')), may hold values from 1 to 8
- l2l_op: bfloat16 [289, 289], replicated, may hold values from -0.375 to 0.375
- p2l_op: bfloat16 [289, 128], replicated, may hold values from -0.5 to 0.5
- target_coords: float32 [2, 4, 262144], P(None, None, ('box', 'ctr')), may hold values from -1 to 1
Outputs:
- potential: float32 [4, 262144], P(None, ('box', 'ctr'))
The draws below stay inside these ranges and needn't reach their ends.
Inputs may be any that keep to these rules, and one draw needn't show every extreme that they name: `centre_box`: Non-decreasing over the centres of one index of box. The centres of box index b name boxes of shard b (boxes b * 2048 to (b + 1) * 2048 - 1) and, a few at its end, boxes among the first 2048 // 32 (at least one) of shard b + 1. `centre_near`: slots at or beyond a centre's near_count are to be ignored. For a centre of ctr index q, slots 0 to 6 name panels p with (p - q * 8192 + 8192 // 4) mod 131072 below 12288. Slot 7 of the i-th centre of a device at ctr index q names a panel of ctr index (q + 1 + (i + r) mod (15)) mod 16, with one r for each device. Roughly a seventh of the used slots name panels of another ctr index.
All inputs are finite; a program needn't handle non-finite values.
Results may differ from the reference program's by a relative error of at most 0.0028.
Values may be sent and summed in bfloat16 or wider, within the bound.
A program may use at most 128 MiB of HBM per device.

```python
import jax
import jax.numpy as jnp
from jax import lax

ORDER = 16
COEF = 289
SRC = 128
NEAR = 8
TPC = 4
CTR_DEV = 2048
BOX_DEV = 2048
PAN_DEV = 8192
CENTRES = 262144
BOXES = 16384
PANELS = 131072
N_BOX = 8
N_CTR = 16


def draw_centre_box(key, part):
    key = jax.random.fold_in(key, 11)
    row_centres = N_CTR * CTR_DEV
    spill_boxes = max(1, BOX_DEV // 32)
    offsets = jax.random.randint(key, (N_BOX, row_centres), 0, BOX_DEV + spill_boxes)
    offsets = jnp.sort(offsets, axis=1)
    shard_start = (jnp.arange(N_BOX, dtype=jnp.int32) * BOX_DEV)[:, None]
    boxes = jnp.minimum(shard_start + offsets, BOXES - 1).reshape(-1)
    boxes = boxes.at[0].set(0)
    boxes = boxes.at[-1].set(BOXES - 1)
    return boxes.astype(jnp.int32)


def draw_centre_near(key, part):
    key = jax.random.fold_in(key, 23)
    key_place, key_window, key_shift, key_far = jax.random.split(key, 4)
    centre_index = jnp.arange(CENTRES, dtype=jnp.int32)
    device_index = centre_index // CTR_DEV
    ctr_index = device_index % N_CTR
    local_index = centre_index % CTR_DEV
    stride = PAN_DEV // CTR_DEV
    position = ctr_index * PAN_DEV + local_index * stride + jax.random.randint(key_place, (CENTRES,), 0, stride)
    margin_rows = PAN_DEV // 4
    window = position[None, :] + jax.random.randint(key_window, (NEAR - 1, CENTRES), -margin_rows, margin_rows + 1)
    window = window % PANELS
    shifts = jax.random.randint(key_shift, (N_BOX * N_CTR,), 0, N_CTR - 1)
    offset = 1 + (local_index + shifts[device_index]) % (N_CTR - 1)
    far_owner = (ctr_index + offset) % N_CTR
    far_panel = far_owner * PAN_DEV + jax.random.randint(key_far, (CENTRES,), 0, PAN_DEV)
    lists = jnp.concatenate([window, far_panel[None, :]], axis=0)
    lists = lists.at[0, 0].set(0)
    lists = lists.at[1, 0].set(PANELS - 1)
    return lists.astype(jnp.int32)


def with_ends(result, key, low, high):
    extent = result.shape
    index_at = [jax.random.randint(jax.random.fold_in(key, axis), (), 0, extent[axis]) for axis in range(len(extent))]
    result = result.at[tuple(index_at)].set(low)
    longest = extent.index(max(extent))
    index_at[longest] = (index_at[longest] + 1) % extent[longest]
    return result.at[tuple(index_at)].set(high)


def level_of(stream_key, shape, cuts, least, largest):
    level, own = 1.0, jax.random.fold_in(stream_key, 6)
    for dim, parts in cuts:
        draws = jnp.exp(jax.random.uniform(jax.random.fold_in(own, dim), (parts,), jnp.float32, least / len(cuts), largest / len(cuts)))
        level = level * jnp.repeat(draws, shape[dim] // parts).reshape([-1 if axis == dim else 1 for axis in range(len(shape))])
    return level


def bell_draw(own_key, extent, width, most, cuts=(), kind=jnp.bfloat16):
    array = jax.random.normal(own_key, extent, jnp.float32) * width
    if len(cuts) > 0:
        array = level_of(own_key, extent, cuts, -0.22, 0.18) * array
    return jnp.clip(array, min=-most, max=most).astype(kind)


def setup_inputs(seed: int = 0) -> dict:
    splits = jax.random.split(jax.random.key(seed), 10)
    return {
        "box_locals": bell_draw(splits[0], (COEF, BOXES), 1.0, 6.0, ((1, 8),)),
        "centre_box": draw_centre_box(jax.random.fold_in(splits[9], 71), 0),
        "centre_rho": jnp.clip(0.85 + 0.14999998 * jax.random.uniform(splits[2], (CENTRES,), jnp.float32) ** level_of(splits[2], (CENTRES,), ((0, 128),), -0.2, 0.2), 0.85, 1.0),
        "panel_sources": bell_draw(splits[3], (PANELS, SRC), 1.0, 6.0, ((0, 16),)),
        "centre_near": draw_centre_near(jax.random.fold_in(splits[9], 71), 0),
        "near_count": with_ends(jax.random.randint(splits[5], (CENTRES,), 1, NEAR + 1), jax.random.fold_in(splits[5], 1), 1, NEAR).astype(jnp.int32),
        "l2l_op": bell_draw(splits[6], (COEF, COEF), COEF ** -0.5, 0.375),
        "p2l_op": bell_draw(splits[7], (COEF, SRC), SRC ** -0.5, 0.5),
        "target_coords": jnp.clip(jax.random.uniform(splits[8], (2, TPC, CENTRES), jnp.float32, -1.0, 1.0) * level_of(splits[8], (2, TPC, CENTRES), ((2, 128),), -0.4, 0.0), -1.0, 1.0),
    }


def chebyshev(values, order):
    terms = [jnp.ones_like(values), values]
    for level in range(2, order + 1):
        terms.append(2.0 * values * terms[-1] - terms[-2])
    return jnp.stack(terms[:order + 1])


def degree_table(order):
    steps = jnp.arange(order + 1, dtype=jnp.float32)
    return (steps[:, None] + steps[None, :]).reshape(-1)


def reference(box_locals, centre_box, centre_rho, panel_sources, centre_near, near_count, l2l_op, p2l_op, target_coords):
    near_sum = jnp.zeros((centre_box.shape[0], panel_sources.shape[1]), jnp.float32)
    for slot in range(NEAR):
        rows = panel_sources[centre_near[slot]].astype(jnp.float32)
        near_sum = near_sum + jnp.where((slot < near_count)[:, None], rows, 0.0)
    near_round = near_sum.astype(jnp.bfloat16)
    box_picked = box_locals[:, centre_box]
    scale = jnp.exp(degree_table(ORDER)[:, None] * jnp.log(centre_rho)[None, :])
    translated = jnp.dot(l2l_op, box_picked, preferred_element_type=jnp.float32)
    direct = jnp.einsum('ks,cs->kc', p2l_op, near_round, preferred_element_type=jnp.float32)
    centre_exp = scale * translated + direct
    grid = centre_exp.reshape(ORDER + 1, ORDER + 1, -1)
    cheb_u = chebyshev(target_coords[0], ORDER)
    cheb_v = chebyshev(target_coords[1], ORDER)
    return jnp.einsum('ijc,itc,jtc->tc', grid, cheb_u, cheb_v, precision=lax.Precision.HIGHEST)
```

```python
import functools

import jax
import jax.numpy as jnp
from jax import lax
from jax.experimental import pallas as pl
from jax.experimental.pallas import tpu as pltpu
from jax.sharding import PartitionSpec as P

N_CTR = 16
N_BOX = 8
CTR = 2048
PAN = 8192
MARGIN = 2048
COEF = 289
DEG = 17
SRC = 128
BOXES = 2048
KP = 296
ZERO_ROW = PAN + 2 * MARGIN
TAB = ZERO_ROW + 8
RING = N_CTR - 1
REQ = 2176
FAR = 144
FAR_USED = 137
HALF = MARGIN // 2
BLOCK = 256
UNROLL = 32
MESH = pl.DeviceIdType.MESH
F32 = jnp.float32
BF16 = jnp.bfloat16


def evaluate(grid, table, tile):
    out = []
    for t in range(4):
        acc = None
        for b in range(DEG):
            term = grid[16 * b:16 * b + 16, :] * table[tile, pl.ds(8 * b + 4 + t, 1), :]
            acc = term if acc is None else acc + term
        acc = acc * table[tile, pl.ds(t, 16, stride=8), :]
        last = grid[272:296, :] * table[tile, pl.ds(4 + t, 24, stride=8), :]
        last = last * table[tile, pl.ds(8 * 16 + t, 1), :]
        total = (acc[0:8] + acc[8:16]) + (last[0:8] + last[8:16] + last[16:24])
        out.append(jnp.sum(total, axis=0, keepdims=True))
    return jnp.concatenate(out, axis=0)


def fill(table, xy_ref, rho_ref):
    def one(tile, _):
        lanes = pl.ds(pl.multiple_of(tile * 128, 128), 128)
        x = xy_ref[:, lanes]
        square = None
        if rho_ref is not None:
            rho = rho_ref[:, lanes]
            x, square = x * rho, rho * rho
        before, now = jnp.ones_like(x), x
        table[tile, pl.ds(0, 8), :] = before
        table[tile, pl.ds(8, 8), :] = now
        for n in range(2, DEG):
            later = 2.0 * x * now - (before if square is None else square * before)
            table[tile, pl.ds(8 * n, 8), :] = later
            before, now = now, later
        table[tile, pl.ds(8 * DEG, 56), :] = jnp.zeros((56, 128), F32)
        return 0

    lax.fori_loop(0, CTR // 128, one, 0)


def kernel(
    box_hbm, cbox_ref, rho_ref, pan_hbm, near_ref, count_ref, l2l_ref, p2l_ref, xy_ref,
    out_ref,
    loc, boxv, boxn, prevb, nextb, tab, idx_v, req_v, reqs_v, stage, send_v, far, acc, tplain, tscaled, l2, p2, potb,
    idx_s, req_s,
    loc_sem, margin_send, margin_recv, share_send, share_recv, box_sems, req_send, req_recv, far_send, far_recv, smem_sems,
):
    b, q = lax.axis_index("box"), lax.axis_index("ctr")
    core = lax.rem(b, 2)
    sibling = b + 1 - 2 * core

    def on_ctr(other):
        return (b, other)

    load_pan = pltpu.make_async_copy(pan_hbm, loc, loc_sem.at[0])
    load_box = pltpu.make_async_copy(box_hbm, boxv, loc_sem.at[1])
    load_pan.start()
    load_box.start()

    barrier = pltpu.get_barrier_semaphore()

    def greet(o, _):
        pl.semaphore_signal(barrier, inc=1, device_id=on_ctr(lax.rem(q + o, N_CTR)), device_id_type=MESH)
        return 0

    lax.fori_loop(1, N_CTR, greet, 0)
    for step in (1, N_BOX - 1):
        pl.semaphore_signal(barrier, inc=1, device_id=(lax.rem(b + step, N_BOX), q), device_id_type=MESH)

    slot7 = near_ref[7:8, :]
    count = count_ref[...]
    i = lax.broadcasted_iota(jnp.int32, (1, CTR), 1)
    rem15 = i - 15 * ((i * 34953) >> 19)
    shift = (((slot7 >> 13) - q) & 15) - 1 - rem15
    shift = jnp.where(shift < 0, shift + 15, shift)
    full = count == 8
    r = jnp.clip(jnp.max(jnp.where(full, shift, 0)), 0, 14)
    req_v[0:1, 0:CTR] = jnp.where(full, (slot7 & (PAN - 1)) + MARGIN, ZERO_ROW)
    lane = lax.broadcasted_iota(jnp.int32, (1, REQ - CTR), 1)
    req_v[0:1, CTR:REQ] = jnp.where(lane == REQ - CTR - 1, r, ZERO_ROW)
    near = near_ref[...]
    slot = lax.broadcasted_iota(jnp.int32, (8, CTR), 0)
    idx_v[...] = jnp.where(slot < count, (near - q * PAN + MARGIN) & (N_CTR * PAN - 1), ZERO_ROW)

    pl.semaphore_wait(barrier, RING + 2)

    right, left = lax.rem(q + 1, N_CTR), lax.rem(q + RING, N_CTR)
    my_half = pl.ds(pl.multiple_of(core * HALF, HALF), HALF)
    to_right = pltpu.make_async_remote_copy(
        pan_hbm.at[pl.ds(pl.multiple_of(PAN - MARGIN + core * HALF, HALF), HALF), :], prevb.at[my_half, :],
        margin_send.at[0], margin_recv.at[0], device_id=on_ctr(right), device_id_type=MESH)
    to_left = pltpu.make_async_remote_copy(
        pan_hbm.at[my_half, :], nextb.at[my_half, :],
        margin_send.at[1], margin_recv.at[1], device_id=on_ctr(left), device_id_type=MESH)
    to_right.start()
    to_left.start()
    box_copy = pltpu.make_async_remote_copy(
        box_hbm.at[:, pl.ds(0, 128)], boxn, box_sems.at[0], box_sems.at[1],
        device_id=(lax.rem(b + N_BOX - 1, N_BOX), q), device_id_type=MESH)
    box_copy.start()

    def request(o):
        return pltpu.make_async_remote_copy(
            req_v, reqs_v.at[o - 1], req_send.at[o - 1], req_recv.at[o - 1],
            device_id=on_ctr(lax.rem(q + o, N_CTR)), device_id_type=MESH)

    def ask(o, _):
        request(o).start()
        return 0

    lax.fori_loop(1, N_CTR, ask, 0)

    for j in range(7):
        pltpu.make_async_copy(idx_v.at[j], idx_s.at[pl.ds(j * CTR, CTR)], smem_sems.at[RING + j]).start()

    tab[pl.ds(ZERO_ROW, 8), :] = jnp.zeros((8, SRC), F32)
    load_pan.wait()

    def widen(k, _):
        rows = pl.ds(pl.multiple_of(k * 512, 512), 512)
        tab[pl.ds(pl.multiple_of(MARGIN + k * 512, 512), 512), :] = loc[rows, :].astype(F32)
        return 0

    lax.fori_loop(0, PAN // 512, widen, 0)

    fill(tplain, xy_ref, None)
    fill(tscaled, xy_ref, rho_ref)

    row = lax.broadcasted_iota(jnp.int32, (KP, COEF), 0)
    col = lax.broadcasted_iota(jnp.int32, (KP, COEF), 1)
    source = jnp.where(row < 272, (row & 15) * DEG + (row >> 4), 16 * DEG + row - 272)
    order = (col == source).astype(F32).astype(BF16)
    l2[...] = jnp.dot(order, l2l_ref[...], preferred_element_type=F32).astype(BF16)
    p2[...] = jnp.dot(order, p2l_ref[...], preferred_element_type=F32).astype(BF16)

    def take_request(o, _):
        request(o).wait_recv()
        pltpu.make_async_copy(reqs_v.at[o - 1, 0], req_s.at[pl.ds((o - 1) * REQ, REQ)], smem_sems.at[o - 1]).start()
        return 0

    lax.fori_loop(1, N_CTR, take_request, 0)

    def answer(o):
        return pltpu.make_async_remote_copy(
            send_v.at[o - 1], far.at[o - 1], far_send.at[o - 1], far_recv.at[o - 1],
            device_id=on_ctr(lax.rem(q + N_CTR - o, N_CTR)), device_id_type=MESH)

    def have_request(o, _):
        pltpu.make_async_copy(reqs_v.at[o - 1, 0], req_s.at[pl.ds((o - 1) * REQ, REQ)], smem_sems.at[o - 1]).wait()
        return 0

    lax.fori_loop(1, N_CTR, have_request, 0)

    def serve(o, _):
        base = (o - 1) * REQ
        shift = req_s[base + REQ - 1]
        first = lax.rem(o + 14 - shift, RING)
        mine = req_s.at[pl.ds(base + first, 15 * (FAR_USED - 1) + 1)]
        for k in range(FAR_USED):
            stage[pl.ds(k, 1), :] = tab[pl.ds(mine[15 * k], 1), :]
        send_v[o - 1] = stage[...].astype(BF16)
        answer(o).start()
        return 0

    stage[pl.ds(FAR - 8, 8), :] = jnp.zeros((8, SRC), F32)
    lax.fori_loop(1, N_CTR, serve, 0)

    def share(k, buffer):
        return pltpu.make_async_remote_copy(
            buffer.at[my_half, :], buffer.at[my_half, :], share_send.at[k], share_recv.at[k],
            device_id=(sibling, q), device_id_type=MESH)

    to_right.wait_recv()
    share(0, prevb).start()
    to_left.wait_recv()
    share(1, nextb).start()

    load_box.wait()
    box_copy.wait_recv()

    def box_block(k, _):
        lanes = pl.ds(pl.multiple_of(k * BLOCK, BLOCK), BLOCK)
        offset = cbox_ref[:, lanes] - b * BOXES
        ids = lax.broadcasted_iota(jnp.int32, (BOXES, BLOCK), 0)
        picked = jnp.dot(boxv[...], (ids == offset).astype(F32).astype(BF16), preferred_element_type=F32)
        ids = lax.broadcasted_iota(jnp.int32, (128, BLOCK), 0) + BOXES
        picked += jnp.dot(boxn[...], (ids == offset).astype(F32).astype(BF16), preferred_element_type=F32)
        moved = jnp.dot(l2[...], picked.astype(BF16), preferred_element_type=F32)
        for h in range(BLOCK // 128):
            part = evaluate(moved[:, 128 * h:128 * h + 128], tscaled, k * (BLOCK // 128) + h)
            potb[:, pl.ds(pl.multiple_of(k * BLOCK + 128 * h, 128), 128)] = part
        return 0

    lax.fori_loop(0, CTR // BLOCK, box_block, 0)

    share(0, prevb).wait_recv()
    share(1, nextb).wait_recv()

    def widen_margin(k, _):
        rows = pl.ds(pl.multiple_of(k * 512, 512), 512)
        tab[rows, :] = prevb[rows, :].astype(F32)
        tab[pl.ds(pl.multiple_of(MARGIN + PAN + k * 512, 512), 512), :] = nextb[rows, :].astype(F32)
        return 0

    lax.fori_loop(0, MARGIN // 512, widen_margin, 0)
    for j in range(7):
        pltpu.make_async_copy(idx_v.at[j], idx_s.at[pl.ds(j * CTR, CTR)], smem_sems.at[RING + j]).wait()

    def gather(k, _):
        c0 = k * UNROLL
        lists = [idx_s.at[pl.ds(j * CTR + c0, UNROLL)] for j in range(7)]
        for u in range(UNROLL):
            rows = [tab[pl.ds(lists[j][u], 1), :] for j in range(7)]
            while len(rows) > 1:
                rows = [x + y for x, y in zip(rows[::2], rows[1::2])] + ([rows[-1]] if len(rows) % 2 else [])
            acc[pl.ds(c0 + u, 1), :] = rows[0]
        return 0

    lax.fori_loop(0, CTR // UNROLL, gather, 0)

    def take_far(o, _):
        answer(o).wait_recv()
        return 0

    lax.fori_loop(1, N_CTR, take_far, 0)
    for m in range(RING):
        rows = far[lax.rem(m + r, RING)].astype(F32)
        at = pl.ds(m, FAR, stride=RING)
        acc[at, :] = acc[at, :] + rows

    def near_block(k, _):
        lanes = pl.ds(pl.multiple_of(k * BLOCK, BLOCK), BLOCK)
        near_round = acc[lanes, :].astype(BF16)
        direct = lax.dot_general(p2[...], near_round, (((1,), (1,)), ((), ())), preferred_element_type=F32)
        for h in range(BLOCK // 128):
            part = evaluate(direct[:, 128 * h:128 * h + 128], tplain, k * (BLOCK // 128) + h)
            cols = pl.ds(pl.multiple_of(k * BLOCK + 128 * h, 128), 128)
            out_ref[:, cols] = potb[:, cols] + part
        return 0

    lax.fori_loop(0, CTR // BLOCK, near_block, 0)

    to_right.wait_send()
    to_left.wait_send()
    box_copy.wait_send()
    share(0, prevb).wait_send()
    share(1, nextb).wait_send()

    def finish(o, _):
        request(o).wait_send()
        answer(o).wait_send()
        return 0

    lax.fori_loop(1, N_CTR, finish, 0)


def shards(box_locals, centre_box, centre_rho, panel_sources, centre_near, near_count, l2l_op, p2l_op, target_coords):
    vmem = pl.BlockSpec(memory_space=pltpu.VMEM)
    anywhere = pl.BlockSpec(memory_space=pl.ANY)
    dma = pltpu.SemaphoreType.DMA
    return pl.pallas_call(
        kernel,
        out_shape=jax.ShapeDtypeStruct((4, CTR), F32),
        in_specs=[anywhere, vmem, vmem, anywhere, vmem, vmem, vmem, vmem, vmem],
        out_specs=vmem,
        scratch_shapes=[
            pltpu.VMEM((PAN, SRC), BF16),
            pltpu.VMEM((COEF, BOXES), BF16),
            pltpu.VMEM((COEF, 128), BF16),
            pltpu.VMEM((MARGIN, SRC), BF16),
            pltpu.VMEM((MARGIN, SRC), BF16),
            pltpu.VMEM((TAB, SRC), F32),
            pltpu.VMEM((8, CTR), jnp.int32),
            pltpu.VMEM((1, REQ), jnp.int32),
            pltpu.VMEM((RING, 1, REQ), jnp.int32),
            pltpu.VMEM((FAR, SRC), F32),
            pltpu.VMEM((RING, FAR, SRC), BF16),
            pltpu.VMEM((RING, FAR, SRC), BF16),
            pltpu.VMEM((RING * FAR, SRC), F32),
            pltpu.VMEM((CTR // 128, 192, 128), F32),
            pltpu.VMEM((CTR // 128, 192, 128), F32),
            pltpu.VMEM((KP, COEF), BF16),
            pltpu.VMEM((KP, SRC), BF16),
            pltpu.VMEM((4, CTR), F32),
            pltpu.SMEM((7 * CTR,), jnp.int32),
            pltpu.SMEM((RING * REQ,), jnp.int32),
            dma((2,)), dma((2,)), dma((2,)), dma((2,)), dma((2,)), dma((2,)),
            dma((RING,)), dma((RING,)), dma((RING,)), dma((RING,)), dma((RING + 7,)),
        ],
        compiler_params=pltpu.CompilerParams(collective_id=0, has_side_effects=True, vmem_limit_bytes=60 * 2**20),
        name="qbx",
    )(
        box_locals, centre_box.reshape(1, CTR), centre_rho.reshape(1, CTR), panel_sources, centre_near,
        near_count.reshape(1, CTR), l2l_op, p2l_op, target_coords.reshape(8, CTR),
    )


def solution(mesh):
    in_specs = (
        P(None, "box"),
        P(("box", "ctr")),
        P(("box", "ctr")),
        P("ctr", None),
        P(None, ("box", "ctr")),
        P(("box", "ctr")),
        P(),
        P(),
        P(None, None, ("box", "ctr")),
    )
    out_specs = P(None, ("box", "ctr"))
    return jax.shard_map(shards, mesh=mesh, in_specs=in_specs, out_specs=out_specs, check_vma=False)
```

```python
import functools

import jax
import jax.numpy as jnp
from jax import lax
from jax.experimental import pallas as pl
from jax.experimental.pallas import tpu as pltpu
from jax.sharding import PartitionSpec as P

N_CTR = 16
N_BOX = 8
CTR = 2048
PAN = 8192
MARGIN = 2048
COEF = 289
DEG = 17
SRC = 128
BOXES = 2048
KP = 296
ZERO_ROW = PAN + 2 * MARGIN
TAB = ZERO_ROW + 8
RING = N_CTR - 1
REQ = 256
FAR = 144
FAR_USED = 137
HALF = MARGIN // 2
FAR_ORDER = (5, 6, 7, 9, 10, 11, 13, 14, 15, 1, 2, 3, 4, 8, 12)
BLOCK = 256
UNROLL = 128
MESH = pl.DeviceIdType.MESH
F32 = jnp.float32
BF16 = jnp.bfloat16


def evaluate(grid, table, tile):
    out = []
    for t in range(4):
        acc = None
        for b in range(DEG):
            term = grid[16 * b:16 * b + 16, :] * table[tile, pl.ds(8 * b + 4 + t, 1), :]
            acc = term if acc is None else acc + term
        acc = acc * table[tile, pl.ds(t, 16, stride=8), :]
        last = grid[272:296, :] * table[tile, pl.ds(4 + t, 24, stride=8), :]
        last = last * table[tile, pl.ds(8 * 16 + t, 1), :]
        total = (acc[0:8] + acc[8:16]) + (last[0:8] + last[8:16] + last[16:24])
        out.append(jnp.sum(total, axis=0, keepdims=True))
    return jnp.concatenate(out, axis=0)


def fill(table, xy, rho_ref):
    def one(tile, _):
        lanes = pl.ds(pl.multiple_of(tile * 128, 128), 128)
        x = jnp.concatenate([xy[0, :, lanes], xy[1, :, lanes]], axis=0)
        square = None
        if rho_ref is not None:
            rho = rho_ref[:, lanes]
            x, square = x * rho, rho * rho
        before, now = jnp.ones_like(x), x
        table[tile, pl.ds(0, 8), :] = before
        table[tile, pl.ds(8, 8), :] = now
        for n in range(2, DEG):
            later = 2.0 * x * now - (before if square is None else square * before)
            table[tile, pl.ds(8 * n, 8), :] = later
            before, now = now, later
        table[tile, pl.ds(8 * DEG, 56), :] = jnp.zeros((56, 128), F32)
        return 0

    lax.fori_loop(0, CTR // 128, one, 0)


def kernel(
    box_hbm, cbox_hbm, rho_hbm, pan_hbm, near_hbm, count_hbm, l2l_hbm, p2l_hbm, xy_hbm,
    out_ref,
    boxv, cbox_ref, rho_ref, loc, near_ref, count_ref, l2l_ref, p2l_ref, xy_ref,
    boxs, boxn, prevb, nextb, tab, idx_v, req_v, reqs_v, stage, send_v, far, acc, tplain, tscaled, l2, p2, potb,
    idx_s, req_s,
    load_sems, margin_send, margin_recv, share_send, share_recv, box_sems, req_send, req_recv, far_send, far_recv, smem_sems,
):
    b, q = lax.axis_index("box"), lax.axis_index("ctr")
    core = lax.rem(b, 2)
    sibling = b + 1 - 2 * core

    def on_ctr(other):
        return (b, other)

    barrier = pltpu.get_barrier_semaphore()


    def greet(o, _):
        pl.semaphore_signal(barrier, inc=1, device_id=on_ctr(lax.rem(q + o, N_CTR)), device_id_type=MESH)
        return 0

    lax.fori_loop(1, N_CTR, greet, 0)
    for step in (1, N_BOX - 1):
        pl.semaphore_signal(barrier, inc=1, device_id=(lax.rem(b + step, N_BOX), q), device_id_type=MESH)

    loads = [
        pltpu.make_async_copy(source, target, load_sems.at[k])
        for k, (source, target) in enumerate([
            (near_hbm, near_ref), (count_hbm, count_ref), (pan_hbm, loc), (xy_hbm, xy_ref), (rho_hbm, rho_ref),
            (l2l_hbm, l2l_ref), (p2l_hbm, p2l_ref), (cbox_hbm, cbox_ref), (box_hbm, boxv),
            (box_hbm.at[:, pl.ds(0, 128)], boxs)])
    ]
    for load in loads:
        load.start()

    loads[0].wait()
    loads[1].wait()
    slot7 = near_ref[7:8, :]
    count = count_ref[...]
    i = lax.broadcasted_iota(jnp.int32, (1, CTR), 1)
    rem15 = i - 15 * ((i * 34953) >> 19)
    shift = (((slot7 >> 13) - q) & 15) - 1 - rem15
    shift = jnp.where(shift < 0, shift + 15, shift)
    full = count == 8
    r = jnp.clip(jnp.max(jnp.where(full, shift, 0)), 0, 14)
    below = jnp.where(full, ZERO_ROW - MARGIN - (slot7 & (PAN - 1)), 0)
    turn = rem15 + r
    turn = jnp.where(turn >= RING, turn - RING, turn)
    mine = turn == lax.broadcasted_iota(jnp.int32, (16, CTR), 0)
    high = jnp.where(mine, (below >> 7).astype(F32), 0.0)
    low = jnp.where(mine, (below & 127).astype(F32), 0.0)
    place = lax.broadcasted_iota(jnp.int32, (REQ, CTR), 0) == ((i * 34953) >> 19)
    lists = lax.dot_general(
        jnp.concatenate([high, low], axis=0).astype(BF16), place.astype(F32).astype(BF16),
        (((1,), (1,)), ((), ())), preferred_element_type=F32).astype(jnp.int32)
    lists = jnp.clip(ZERO_ROW - (lists[0:16] * 128 + lists[16:32]), 0, ZERO_ROW)
    for o in range(1, N_CTR):
        req_v[o - 1] = lists[o - 1:o]
    slot = lax.broadcasted_iota(jnp.int32, (8, CTR), 0)
    idx_v[...] = jnp.where(slot < count, (near_ref[...] - q * PAN + MARGIN) & (N_CTR * PAN - 1), ZERO_ROW)
    to_smem = [pltpu.make_async_copy(idx_v.at[j], idx_s.at[pl.ds(j * CTR, CTR)], smem_sems.at[RING + j]) for j in range(7)]
    for copy in to_smem:
        copy.start()

    pl.semaphore_wait(barrier, RING + 2)

    def request(o):
        return pltpu.make_async_remote_copy(
            req_v.at[o - 1], reqs_v.at[o - 1], req_send.at[o - 1], req_recv.at[o - 1],
            device_id=on_ctr(lax.rem(q + o, N_CTR)), device_id_type=MESH)

    for o in FAR_ORDER:
        request(o).start()

    margins = []
    for k, (buffer, step, start) in enumerate(((prevb, 1, PAN - MARGIN), (nextb, RING, 0))):
        half = pl.ds(pl.multiple_of(core * HALF, HALF), HALF)
        fetch = pltpu.make_async_remote_copy(
            pan_hbm.at[pl.ds(pl.multiple_of(start + core * HALF, HALF), HALF), :], buffer.at[half, :],
            margin_send.at[k], margin_recv.at[k], device_id=on_ctr(lax.rem(q + step, N_CTR)), device_id_type=MESH)
        share = pltpu.make_async_remote_copy(
            buffer.at[half, :], buffer.at[half, :], share_send.at[k], share_recv.at[k],
            device_id=(sibling, q), device_id_type=MESH)
        margins.append((fetch, share))
    for fetch, _ in margins:
        fetch.start()

    box_copy = pltpu.make_async_remote_copy(
        boxs, boxn, box_sems.at[0], box_sems.at[1],
        device_id=(lax.rem(b + N_BOX - 1, N_BOX), q), device_id_type=MESH)
    loads[9].wait()
    box_copy.start()
    tab[pl.ds(ZERO_ROW, 8), :] = jnp.zeros((8, SRC), F32)
    loads[2].wait()

    def widen(k, _):
        rows = pl.ds(pl.multiple_of(k * 512, 512), 512)
        tab[pl.ds(pl.multiple_of(MARGIN + k * 512, 512), 512), :] = loc[rows, :].astype(F32)
        return 0

    lax.fori_loop(0, PAN // 512, widen, 0)
    loads[3].wait()
    loads[4].wait()
    fill(tplain, xy_ref, None)
    fill(tscaled, xy_ref, rho_ref)
    loads[5].wait()
    loads[6].wait()
    row = lax.broadcasted_iota(jnp.int32, (KP, COEF), 0)
    col = lax.broadcasted_iota(jnp.int32, (KP, COEF), 1)
    source = jnp.where(row < 272, (row & 15) * DEG + (row >> 4), 16 * DEG + row - 272)
    order = (col == source).astype(F32).astype(BF16)
    l2[...] = jnp.dot(order, l2l_ref[...], preferred_element_type=F32).astype(BF16)
    p2[...] = jnp.dot(order, p2l_ref[...], preferred_element_type=F32).astype(BF16)

    def list_copy(o):
        return pltpu.make_async_copy(reqs_v.at[o - 1, 0], req_s.at[pl.ds((o - 1) * REQ, REQ)], smem_sems.at[o - 1])

    def take_request(o, _):
        request(o).wait_recv()
        list_copy(o).start()
        return 0

    lax.fori_loop(1, N_CTR, take_request, 0)

    def have_request(o, _):
        list_copy(o).wait()
        return 0

    lax.fori_loop(1, N_CTR, have_request, 0)

    def answer(o):
        return pltpu.make_async_remote_copy(
            send_v.at[o - 1], far.at[o - 1], far_send.at[o - 1], far_recv.at[o - 1],
            device_id=on_ctr(lax.rem(q + N_CTR - o, N_CTR)), device_id_type=MESH)

    def serve(k, _):
        o = 4 * lax.rem(k // 3 + 1, 4) + 1 + lax.rem(k, 3)
        serve_one(o)
        return 0

    def serve_column(k, _):
        serve_one(4 * k)
        return 0

    def serve_one(o):
        base = (o - 1) * REQ
        mine = req_s.at[pl.ds(base, FAR_USED)]
        for k in range(FAR_USED):
            stage[pl.ds(k, 1), :] = tab[pl.ds(mine[k], 1), :]
        send_v[o - 1] = stage[...].astype(BF16)

    stage[pl.ds(FAR - 8, 8), :] = jnp.zeros((8, SRC), F32)
    lax.fori_loop(0, 12, serve, 0)
    lax.fori_loop(1, 4, serve_column, 0)

    for fetch, share in margins:
        fetch.wait_recv()
        share.start()
    for o in FAR_ORDER:
        answer(o).start()

    loads[7].wait()
    loads[8].wait()
    box_copy.wait_recv()

    def box_block(k, _):
        lanes = pl.ds(pl.multiple_of(k * BLOCK, BLOCK), BLOCK)
        offset = cbox_ref[:, lanes] - b * BOXES
        ids = lax.broadcasted_iota(jnp.int32, (BOXES, BLOCK), 0)
        picked = jnp.dot(boxv[...], (ids == offset).astype(F32).astype(BF16), preferred_element_type=F32)
        ids = lax.broadcasted_iota(jnp.int32, (128, BLOCK), 0) + BOXES
        picked += jnp.dot(boxn[...], (ids == offset).astype(F32).astype(BF16), preferred_element_type=F32)
        moved = jnp.dot(l2[...], picked.astype(BF16), preferred_element_type=F32)
        for h in range(BLOCK // 128):
            part = evaluate(moved[:, 128 * h:128 * h + 128], tscaled, k * (BLOCK // 128) + h)
            potb[:, pl.ds(pl.multiple_of(k * BLOCK + 128 * h, 128), 128)] = part
        return 0

    lax.fori_loop(0, CTR // BLOCK, box_block, 0)

    for _, share in margins:
        share.wait_recv()

    def widen_margin(k, _):
        rows = pl.ds(pl.multiple_of(k * 512, 512), 512)
        tab[rows, :] = prevb[rows, :].astype(F32)
        tab[pl.ds(pl.multiple_of(MARGIN + PAN + k * 512, 512), 512), :] = nextb[rows, :].astype(F32)
        return 0

    lax.fori_loop(0, MARGIN // 512, widen_margin, 0)
    for copy in to_smem:
        copy.wait()

    def gather(k, _):
        c0 = k * UNROLL
        lists = [idx_s.at[pl.ds(j * CTR + c0, UNROLL)] for j in range(7)]
        for u in range(UNROLL):
            rows = [tab[pl.ds(lists[j][u], 1), :] for j in range(7)]
            while len(rows) > 1:
                rows = [x + y for x, y in zip(rows[::2], rows[1::2])] + ([rows[-1]] if len(rows) % 2 else [])
            acc[pl.ds(c0 + u, 1), :] = rows[0]
        return 0

    lax.fori_loop(0, CTR // UNROLL, gather, 0)

    def take_far(o, _):
        answer(o).wait_recv()
        return 0

    lax.fori_loop(1, N_CTR, take_far, 0)
    for m in range(RING):
        rows = far[lax.rem(m + r, RING)].astype(F32)
        at = pl.ds(m, FAR, stride=RING)
        acc[at, :] = acc[at, :] + rows

    def near_block(k, _):
        lanes = pl.ds(pl.multiple_of(k * BLOCK, BLOCK), BLOCK)
        near_round = acc[lanes, :].astype(BF16)
        direct = lax.dot_general(p2[...], near_round, (((1,), (1,)), ((), ())), preferred_element_type=F32)
        for h in range(BLOCK // 128):
            part = evaluate(direct[:, 128 * h:128 * h + 128], tplain, k * (BLOCK // 128) + h)
            cols = pl.ds(pl.multiple_of(k * BLOCK + 128 * h, 128), 128)
            out_ref[:, cols] = potb[:, cols] + part
        return 0

    lax.fori_loop(0, CTR // BLOCK, near_block, 0)

    box_copy.wait_send()
    for group in margins:
        for copy in group:
            copy.wait_send()

    def finish(o, _):
        request(o).wait_send()
        answer(o).wait_send()
        return 0

    lax.fori_loop(1, N_CTR, finish, 0)


def shards(box_locals, centre_box, centre_rho, panel_sources, centre_near, near_count, l2l_op, p2l_op, target_coords):
    vmem = pl.BlockSpec(memory_space=pltpu.VMEM)
    anywhere = pl.BlockSpec(memory_space=pl.ANY)
    dma = pltpu.SemaphoreType.DMA
    return pl.pallas_call(
        kernel,
        out_shape=jax.ShapeDtypeStruct((4, CTR), F32),
        in_specs=[anywhere] * 9,
        out_specs=vmem,
        scratch_shapes=[
            pltpu.VMEM((COEF, BOXES), BF16),
            pltpu.VMEM((1, CTR), jnp.int32),
            pltpu.VMEM((1, CTR), F32),
            pltpu.VMEM((PAN, SRC), BF16),
            pltpu.VMEM((8, CTR), jnp.int32),
            pltpu.VMEM((1, CTR), jnp.int32),
            pltpu.VMEM((COEF, COEF), BF16),
            pltpu.VMEM((COEF, SRC), BF16),
            pltpu.VMEM((2, 4, CTR), F32),
            pltpu.VMEM((COEF, 128), BF16),
            pltpu.VMEM((COEF, 128), BF16),
            pltpu.VMEM((MARGIN, SRC), BF16),
            pltpu.VMEM((MARGIN, SRC), BF16),
            pltpu.VMEM((TAB, SRC), F32),
            pltpu.VMEM((8, CTR), jnp.int32),
            pltpu.VMEM((RING, 1, REQ), jnp.int32),
            pltpu.VMEM((RING, 1, REQ), jnp.int32),
            pltpu.VMEM((FAR, SRC), F32),
            pltpu.VMEM((RING, FAR, SRC), BF16),
            pltpu.VMEM((RING, FAR, SRC), BF16),
            pltpu.VMEM((RING * FAR, SRC), F32),
            pltpu.VMEM((CTR // 128, 192, 128), F32),
            pltpu.VMEM((CTR // 128, 192, 128), F32),
            pltpu.VMEM((KP, COEF), BF16),
            pltpu.VMEM((KP, SRC), BF16),
            pltpu.VMEM((4, CTR), F32),
            pltpu.SMEM((7 * CTR,), jnp.int32),
            pltpu.SMEM((RING * REQ,), jnp.int32),
            dma((10,)), dma((2,)), dma((2,)), dma((2,)), dma((2,)), dma((2,)),
            dma((RING,)), dma((RING,)), dma((RING,)), dma((RING,)), dma((RING + 7,)),
        ],
        compiler_params=pltpu.CompilerParams(collective_id=0, has_side_effects=True, vmem_limit_bytes=60 * 2**20),
        name="qbx",
    )(
        box_locals, centre_box.reshape(1, CTR), centre_rho.reshape(1, CTR), panel_sources, centre_near,
        near_count.reshape(1, CTR), l2l_op, p2l_op, target_coords,
    )


def solution(mesh):
    in_specs = (
        P(None, "box"),
        P(("box", "ctr")),
        P(("box", "ctr")),
        P("ctr", None),
        P(None, ("box", "ctr")),
        P(("box", "ctr")),
        P(),
        P(),
        P(None, None, ("box", "ctr")),
    )
    out_specs = P(None, ("box", "ctr"))
    return jax.shard_map(shards, mesh=mesh, in_specs=in_specs, out_specs=out_specs, check_vma=False)
```

```python
import itertools

import functools

import jax
import jax.numpy as jnp
from jax import lax
from jax.experimental import pallas as pl
from jax.experimental.pallas import tpu as pltpu
from jax.sharding import PartitionSpec as P

N_CTR = 16
N_BOX = 8
CTR = 2048
PAN = 8192
MARGIN = 2048
COEF = 289
DEG = 17
SRC = 128
BOXES = 2048
KP = 296
ZERO_ROW = PAN + 2 * MARGIN
TAB = ZERO_ROW + 8
RING = N_CTR - 1
REQ = 256
FAR = 144
FAR_USED = 137
HALF = MARGIN // 2
FAR_ORDER = (5, 6, 7, 9, 10, 11, 13, 14, 15, 1, 2, 3, 4, 8, 12)
BLOCK = 256
BLOCKS = CTR // BLOCK
PICKS = 4
SPACING = 14
MESH = pl.DeviceIdType.MESH
F32 = jnp.float32
BF16 = jnp.bfloat16


def evaluate(grid, table, tile):
    return jnp.concatenate([evaluate_one(grid, table, tile, t) for t in range(4)], axis=0)


def evaluate_one(grid, table, tile, t):
    if True:
        acc = None
        for b in range(DEG):
            term = grid[16 * b:16 * b + 16, :] * table[tile, pl.ds(8 * b + 4 + t, 1), :]
            acc = term if acc is None else acc + term
        acc = acc * table[tile, pl.ds(t, 16, stride=8), :]
        last = grid[272:296, :] * table[tile, pl.ds(4 + t, 24, stride=8), :]
        last = last * table[tile, pl.ds(8 * 16 + t, 1), :]
        total = (acc[0:8] + acc[8:16]) + (last[0:8] + last[8:16] + last[16:24])
        return jnp.sum(total, axis=0, keepdims=True)


def fill(table, xy, rho_ref):
    def one(tile, _):
        lanes = pl.ds(pl.multiple_of(tile * 128, 128), 128)
        x = jnp.concatenate([xy[0, :, lanes], xy[1, :, lanes]], axis=0)
        square = None
        if rho_ref is not None:
            rho = rho_ref[:, lanes]
            x, square = x * rho, rho * rho
        before, now = jnp.ones_like(x), x
        table[tile, pl.ds(0, 8), :] = before
        table[tile, pl.ds(8, 8), :] = now
        for n in range(2, DEG):
            later = 2.0 * x * now - (before if square is None else square * before)
            table[tile, pl.ds(8 * n, 8), :] = later
            before, now = now, later
        table[tile, pl.ds(8 * DEG, 56), :] = jnp.zeros((56, 128), F32)
        return 0

    lax.fori_loop(0, CTR // 128, one, 0)


def kernel(
    box_hbm, cbox_hbm, rho_hbm, pan_hbm, near_hbm, count_hbm, l2l_hbm, p2l_hbm, xy_hbm,
    out_ref,
    boxv, cbox_ref, rho_ref, loc, near_ref, count_ref, l2l_ref, p2l_ref, xy_ref,
    boxs, boxn, prevb, nextb, tab, idx_v, req_v, reqs_v, stage, send_v, far, acc, tplain, tscaled, l2, p2, potb,
    idx_s, req_s,
    load_sems, margin_send, margin_recv, share_send, share_recv, box_sems, req_send, req_recv, far_send, far_recv, smem_sems,
):
    b, q = lax.axis_index("box"), lax.axis_index("ctr")
    core = lax.rem(b, 2)
    sibling = b + 1 - 2 * core

    def on_ctr(other):
        return (b, other)

    barrier = pltpu.get_barrier_semaphore()


    def greet(o, _):
        pl.semaphore_signal(barrier, inc=1, device_id=on_ctr(lax.rem(q + o, N_CTR)), device_id_type=MESH)
        return 0

    lax.fori_loop(1, N_CTR, greet, 0)
    for step in (1, N_BOX - 1):
        pl.semaphore_signal(barrier, inc=1, device_id=(lax.rem(b + step, N_BOX), q), device_id_type=MESH)

    loads = [
        pltpu.make_async_copy(source, target, load_sems.at[k])
        for k, (source, target) in enumerate([
            (near_hbm, near_ref), (count_hbm, count_ref), (pan_hbm, loc), (xy_hbm, xy_ref), (rho_hbm, rho_ref),
            (l2l_hbm, l2l_ref), (p2l_hbm, p2l_ref), (cbox_hbm, cbox_ref), (box_hbm, boxv),
            (box_hbm.at[:, pl.ds(0, 128)], boxs)])
    ]
    for load in loads:
        load.start()

    loads[0].wait()
    loads[1].wait()
    slot7 = near_ref[7:8, :]
    count = count_ref[...]
    i = lax.broadcasted_iota(jnp.int32, (1, CTR), 1)
    rem15 = i - 15 * ((i * 34953) >> 19)
    shift = (((slot7 >> 13) - q) & 15) - 1 - rem15
    shift = jnp.where(shift < 0, shift + 15, shift)
    full = count == 8
    r = jnp.clip(jnp.max(jnp.where(full, shift, 0)), 0, 14)
    below = jnp.where(full, ZERO_ROW - MARGIN - (slot7 & (PAN - 1)), 0)
    turn = rem15 + r
    turn = jnp.where(turn >= RING, turn - RING, turn)
    mine = turn == lax.broadcasted_iota(jnp.int32, (16, CTR), 0)
    high = jnp.where(mine, (below >> 7).astype(F32), 0.0)
    low = jnp.where(mine, (below & 127).astype(F32), 0.0)
    place = lax.broadcasted_iota(jnp.int32, (REQ, CTR), 0) == ((i * 34953) >> 19)
    lists = lax.dot_general(
        jnp.concatenate([high, low], axis=0).astype(BF16), place.astype(F32).astype(BF16),
        (((1,), (1,)), ((), ())), preferred_element_type=F32).astype(jnp.int32)
    lists = jnp.clip(ZERO_ROW - (lists[0:16] * 128 + lists[16:32]), 0, ZERO_ROW)
    for o in range(1, N_CTR):
        req_v[o - 1] = lists[o - 1:o]
    slot = lax.broadcasted_iota(jnp.int32, (8, CTR), 0)
    idx_v[...] = jnp.where(slot < count, (near_ref[...] - q * PAN + MARGIN) & (N_CTR * PAN - 1), ZERO_ROW)
    to_smem = [pltpu.make_async_copy(idx_v.at[j], idx_s.at[pl.ds(j * CTR, CTR)], smem_sems.at[RING + j]) for j in range(7)]
    for copy in to_smem:
        copy.start()

    pl.semaphore_wait(barrier, RING + 2)

    def request(o):
        return pltpu.make_async_remote_copy(
            req_v.at[o - 1], reqs_v.at[o - 1], req_send.at[o - 1], req_recv.at[o - 1],
            device_id=on_ctr(lax.rem(q + o, N_CTR)), device_id_type=MESH)

    for o in FAR_ORDER:
        request(o).start()

    margins = []
    for k, (buffer, step, start) in enumerate(((prevb, 1, PAN - MARGIN), (nextb, RING, 0))):
        half = pl.ds(pl.multiple_of(core * HALF, HALF), HALF)
        fetch = pltpu.make_async_remote_copy(
            pan_hbm.at[pl.ds(pl.multiple_of(start + core * HALF, HALF), HALF), :], buffer.at[half, :],
            margin_send.at[k], margin_recv.at[k], device_id=on_ctr(lax.rem(q + step, N_CTR)), device_id_type=MESH)
        share = pltpu.make_async_remote_copy(
            buffer.at[half, :], buffer.at[half, :], share_send.at[k], share_recv.at[k],
            device_id=(sibling, q), device_id_type=MESH)
        margins.append((fetch, share))
    for fetch, _ in margins:
        fetch.start()

    box_copy = pltpu.make_async_remote_copy(
        boxs, boxn, box_sems.at[0], box_sems.at[1],
        device_id=(lax.rem(b + N_BOX - 1, N_BOX), q), device_id_type=MESH)
    loads[9].wait()
    box_copy.start()
    tab[pl.ds(ZERO_ROW, 8), :] = jnp.zeros((8, SRC), F32)
    loads[2].wait()

    def widen(k, _):
        rows = pl.ds(pl.multiple_of(k * 512, 512), 512)
        tab[pl.ds(pl.multiple_of(MARGIN + k * 512, 512), 512), :] = loc[rows, :].astype(F32)
        return 0

    lax.fori_loop(0, PAN // 512, widen, 0)
    loads[3].wait()
    loads[4].wait()
    fill(tplain, xy_ref, None)
    fill(tscaled, xy_ref, rho_ref)
    loads[5].wait()
    loads[6].wait()
    row = lax.broadcasted_iota(jnp.int32, (KP, COEF), 0)
    col = lax.broadcasted_iota(jnp.int32, (KP, COEF), 1)
    source = jnp.where(row < 272, (row & 15) * DEG + (row >> 4), 16 * DEG + row - 272)
    order = (col == source).astype(F32).astype(BF16)
    l2[...] = jnp.dot(order, l2l_ref[...], preferred_element_type=F32).astype(BF16)
    p2[...] = jnp.dot(order, p2l_ref[...], preferred_element_type=F32).astype(BF16)

    def list_copy(o):
        return pltpu.make_async_copy(reqs_v.at[o - 1, 0], req_s.at[pl.ds((o - 1) * REQ, REQ)], smem_sems.at[o - 1])

    def take_request(o, _):
        request(o).wait_recv()
        list_copy(o).start()
        return 0

    lax.fori_loop(1, N_CTR, take_request, 0)

    def have_request(o, _):
        list_copy(o).wait()
        return 0

    lax.fori_loop(1, N_CTR, have_request, 0)

    def answer(o):
        return pltpu.make_async_remote_copy(
            send_v.at[o - 1], far.at[o - 1], far_send.at[o - 1], far_recv.at[o - 1],
            device_id=on_ctr(lax.rem(q + N_CTR - o, N_CTR)), device_id_type=MESH)

    def serve(k, _):
        o = 4 * lax.rem(k // 3 + 1, 4) + 1 + lax.rem(k, 3)
        serve_one(o)
        return 0

    def serve_column(k, _):
        serve_one(4 * k)
        return 0

    def serve_one(o):
        base = (o - 1) * REQ
        mine = req_s.at[pl.ds(base, FAR_USED)]
        for k in range(FAR_USED):
            stage[pl.ds(k, 1), :] = tab[pl.ds(mine[k], 1), :]
        send_v[o - 1] = stage[...].astype(BF16)

    stage[pl.ds(FAR - 8, 8), :] = jnp.zeros((8, SRC), F32)
    lax.fori_loop(0, 12, serve, 0)
    lax.fori_loop(1, 4, serve_column, 0)

    for fetch, share in margins:
        fetch.wait_recv()
        share.start()
    for o in FAR_ORDER:
        answer(o).start()

    loads[7].wait()
    loads[8].wait()
    box_copy.wait_recv()

    def box_steps(k):
        lanes = pl.ds(pl.multiple_of(k * BLOCK, BLOCK), BLOCK)
        offset = cbox_ref[:, lanes] - b * BOXES
        width = BOXES // PICKS
        picked = None
        for n in range(PICKS):
            ids = lax.broadcasted_iota(jnp.int32, (width, BLOCK), 0) + n * width
            term = jnp.dot(boxv[:, n * width:n * width + width], (ids == offset).astype(F32).astype(BF16), preferred_element_type=F32)
            picked = term if picked is None else picked + term
            yield
        ids = lax.broadcasted_iota(jnp.int32, (128, BLOCK), 0) + BOXES
        picked += jnp.dot(boxn[...], (ids == offset).astype(F32).astype(BF16), preferred_element_type=F32)
        yield
        moved = jnp.dot(l2[...], picked.astype(BF16), preferred_element_type=F32)
        yield
        for h in range(BLOCK // 128):
            cols = pl.ds(pl.multiple_of(k * BLOCK + 128 * h, 128), 128)
            for t in range(4):
                potb[t:t + 1, cols] = evaluate_one(moved[:, 128 * h:128 * h + 128], tscaled, k * (BLOCK // 128) + h, t)
                yield

    def box_only(k, _):
        for _ in box_steps(k):
            pass
        return 0

    lax.fori_loop(0, BLOCKS // 2, box_only, 0)

    for _, share in margins:
        share.wait_recv()

    def widen_margin(k, _):
        rows = pl.ds(pl.multiple_of(k * 512, 512), 512)
        tab[rows, :] = prevb[rows, :].astype(F32)
        tab[pl.ds(pl.multiple_of(MARGIN + PAN + k * 512, 512), 512), :] = nextb[rows, :].astype(F32)
        return 0

    lax.fori_loop(0, MARGIN // 512, widen_margin, 0)
    for copy in to_smem:
        copy.wait()

    def tail_steps(k):
        near_round = acc[pl.ds(pl.multiple_of(k * BLOCK, BLOCK), BLOCK), :].astype(BF16)
        direct = lax.dot_general(p2[...], near_round, (((1,), (1,)), ((), ())), preferred_element_type=F32)
        yield
        for h in range(BLOCK // 128):
            cols = pl.ds(pl.multiple_of(k * BLOCK + 128 * h, 128), 128)
            for t in range(4):
                part = evaluate_one(direct[:, 128 * h:128 * h + 128], tplain, k * (BLOCK // 128) + h, t)
                out_ref[t:t + 1, cols] = potb[t:t + 1, cols] + part
                yield

    def gather(k, add, steps):
        c0 = k * BLOCK
        lists = [idx_s.at[pl.ds(j * CTR + c0, BLOCK)] for j in range(7)]
        for u in range(BLOCK):
            if u % SPACING == 0:
                next(steps, None)
            rows = [tab[pl.ds(lists[j][u], 1), :] for j in range(7)]
            if add:
                rows.append(acc[pl.ds(c0 + u, 1), :])
            while len(rows) > 1:
                rows = [x + y for x, y in zip(rows[::2], rows[1::2])] + ([rows[-1]] if len(rows) % 2 else [])
            acc[pl.ds(c0 + u, 1), :] = rows[0]
        for _ in steps:
            pass

    def early(k, _):
        gather(k, False, box_steps(k + BLOCKS // 2))
        return 0

    def late(k, _):
        gather(k, True, itertools.chain(tail_steps(k - BLOCKS // 2), tail_steps(k - 1)))
        return 0

    lax.fori_loop(0, BLOCKS // 2, early, 0)

    def take_far(o, _):
        answer(o).wait_recv()
        return 0

    lax.fori_loop(1, N_CTR, take_far, 0)
    acc[pl.ds(CTR // 2, RING * FAR - CTR // 2), :] = jnp.zeros((RING * FAR - CTR // 2, SRC), F32)
    for m in range(RING):
        rows = far[lax.rem(m + r, RING)].astype(F32)
        at = pl.ds(m, FAR, stride=RING)
        acc[at, :] = acc[at, :] + rows
    lax.fori_loop(BLOCKS // 2, BLOCKS, late, 0)
    for _ in tail_steps(BLOCKS - 1):
        pass

    box_copy.wait_send()
    for group in margins:
        for copy in group:
            copy.wait_send()

    def finish(o, _):
        request(o).wait_send()
        answer(o).wait_send()
        return 0

    lax.fori_loop(1, N_CTR, finish, 0)


def shards(box_locals, centre_box, centre_rho, panel_sources, centre_near, near_count, l2l_op, p2l_op, target_coords):
    vmem = pl.BlockSpec(memory_space=pltpu.VMEM)
    anywhere = pl.BlockSpec(memory_space=pl.ANY)
    dma = pltpu.SemaphoreType.DMA
    return pl.pallas_call(
        kernel,
        out_shape=jax.ShapeDtypeStruct((4, CTR), F32),
        in_specs=[anywhere] * 9,
        out_specs=vmem,
        scratch_shapes=[
            pltpu.VMEM((COEF, BOXES), BF16),
            pltpu.VMEM((1, CTR), jnp.int32),
            pltpu.VMEM((1, CTR), F32),
            pltpu.VMEM((PAN, SRC), BF16),
            pltpu.VMEM((8, CTR), jnp.int32),
            pltpu.VMEM((1, CTR), jnp.int32),
            pltpu.VMEM((COEF, COEF), BF16),
            pltpu.VMEM((COEF, SRC), BF16),
            pltpu.VMEM((2, 4, CTR), F32),
            pltpu.VMEM((COEF, 128), BF16),
            pltpu.VMEM((COEF, 128), BF16),
            pltpu.VMEM((MARGIN, SRC), BF16),
            pltpu.VMEM((MARGIN, SRC), BF16),
            pltpu.VMEM((TAB, SRC), F32),
            pltpu.VMEM((8, CTR), jnp.int32),
            pltpu.VMEM((RING, 1, REQ), jnp.int32),
            pltpu.VMEM((RING, 1, REQ), jnp.int32),
            pltpu.VMEM((FAR, SRC), F32),
            pltpu.VMEM((RING, FAR, SRC), BF16),
            pltpu.VMEM((RING, FAR, SRC), BF16),
            pltpu.VMEM((RING * FAR, SRC), F32),
            pltpu.VMEM((CTR // 128, 192, 128), F32),
            pltpu.VMEM((CTR // 128, 192, 128), F32),
            pltpu.VMEM((KP, COEF), BF16),
            pltpu.VMEM((KP, SRC), BF16),
            pltpu.VMEM((4, CTR), F32),
            pltpu.SMEM((7 * CTR,), jnp.int32),
            pltpu.SMEM((RING * REQ,), jnp.int32),
            dma((10,)), dma((2,)), dma((2,)), dma((2,)), dma((2,)), dma((2,)),
            dma((RING,)), dma((RING,)), dma((RING,)), dma((RING,)), dma((RING + 7,)),
        ],
        compiler_params=pltpu.CompilerParams(collective_id=0, has_side_effects=True, vmem_limit_bytes=60 * 2**20),
        name="qbx",
    )(
        box_locals, centre_box.reshape(1, CTR), centre_rho.reshape(1, CTR), panel_sources, centre_near,
        near_count.reshape(1, CTR), l2l_op, p2l_op, target_coords,
    )


def solution(mesh):
    in_specs = (
        P(None, "box"),
        P(("box", "ctr")),
        P(("box", "ctr")),
        P("ctr", None),
        P(None, ("box", "ctr")),
        P(("box", "ctr")),
        P(),
        P(),
        P(None, None, ("box", "ctr")),
    )
    out_specs = P(None, ("box", "ctr"))
    return jax.shard_map(shards, mesh=mesh, in_specs=in_specs, out_specs=out_specs, check_vma=False)
```

```python
import itertools

import functools

import jax
import jax.numpy as jnp
from jax import lax
from jax.experimental import pallas as pl
from jax.experimental.pallas import tpu as pltpu
from jax.sharding import PartitionSpec as P

N_CTR = 16
N_BOX = 8
CTR = 2048
PAN = 8192
MARGIN = 2048
COEF = 289
DEG = 17
SRC = 128
BOXES = 2048
KP = 296
ZERO_ROW = PAN + 2 * MARGIN
TAB = ZERO_ROW + 8
RING = N_CTR - 1
REQ = 256
FAR = 144
FAR_USED = 137
HALF = MARGIN // 2
FAR_ORDER = (5, 6, 7, 9, 10, 11, 13, 14, 15, 1, 2, 3, 4, 8, 12)
BLOCK = 256
BLOCKS = CTR // BLOCK
PICKS = 4
AHEAD = 1
FIRST = 5
SPACING = 14
MESH = pl.DeviceIdType.MESH
F32 = jnp.float32
BF16 = jnp.bfloat16


def evaluate(grid, table, tile):
    return jnp.concatenate([evaluate_one(grid, table, tile, t) for t in range(4)], axis=0)


def evaluate_one(grid, table, tile, t):
    acc = None
    for b in range(DEG):
        term = grid[16 * b:16 * b + 16, :] * table[tile, pl.ds(8 * b + 4 + t, 1), :]
        acc = term if acc is None else acc + term
    acc = acc * table[tile, pl.ds(t, 16, stride=8), :]
    last = grid[272:296, :] * table[tile, pl.ds(4 + t, 24, stride=8), :]
    last = last * table[tile, pl.ds(8 * 16 + t, 1), :]
    total = (acc[0:8] + acc[8:16]) + (last[0:8] + last[8:16] + last[16:24])
    return jnp.sum(total, axis=0, keepdims=True)


def fill(table, xy, rho_ref):
    def one(tile, _):
        fill_tile(table, xy, rho_ref, tile)
        return 0

    lax.fori_loop(0, CTR // 128, one, 0)


def fill_tile(table, xy, rho_ref, tile):
    lanes = pl.ds(pl.multiple_of(tile * 128, 128), 128)
    x = jnp.concatenate([xy[0, :, lanes], xy[1, :, lanes]], axis=0)
    square = None
    if rho_ref is not None:
        rho = rho_ref[:, lanes]
        x, square = x * rho, rho * rho
    before, now = jnp.ones_like(x), x
    table[tile, pl.ds(0, 8), :] = before
    table[tile, pl.ds(8, 8), :] = now
    for n in range(2, DEG):
        later = 2.0 * x * now - (before if square is None else square * before)
        table[tile, pl.ds(8 * n, 8), :] = later
        before, now = now, later
    table[tile, pl.ds(8 * DEG, 56), :] = jnp.zeros((56, 128), F32)


def kernel(
    box_hbm, cbox_hbm, rho_hbm, pan_hbm, near_hbm, count_hbm, l2l_hbm, p2l_hbm, xy_hbm,
    out_ref,
    boxv, cbox_ref, rho_ref, loc, near_ref, count_ref, l2l_ref, p2l_ref, xy_ref,
    boxs, boxn, prevb, nextb, tab, idx_v, req_v, reqs_v, stage, send_v, far, acc, tplain, tscaled, l2, p2, potb,
    idx_s, req_s,
    load_sems, margin_send, margin_recv, share_send, share_recv, box_sems, req_send, req_recv, far_send, far_recv, smem_sems,
):
    b, q = lax.axis_index("box"), lax.axis_index("ctr")
    core = lax.rem(b, 2)
    sibling = b + 1 - 2 * core

    def on_ctr(other):
        return (b, other)

    barrier = pltpu.get_barrier_semaphore()


    def greet(o, _):
        pl.semaphore_signal(barrier, inc=1, device_id=on_ctr(lax.rem(q + o, N_CTR)), device_id_type=MESH)
        return 0

    lax.fori_loop(1, N_CTR, greet, 0)
    for step in (1, N_BOX - 1):
        pl.semaphore_signal(barrier, inc=1, device_id=(lax.rem(b + step, N_BOX), q), device_id_type=MESH)

    loads = [
        pltpu.make_async_copy(source, target, load_sems.at[k])
        for k, (source, target) in enumerate([
            (near_hbm, near_ref), (count_hbm, count_ref), (pan_hbm, loc), (xy_hbm, xy_ref), (rho_hbm, rho_ref),
            (l2l_hbm, l2l_ref), (p2l_hbm, p2l_ref), (cbox_hbm, cbox_ref), (box_hbm, boxv),
            (box_hbm.at[:, pl.ds(0, 128)], boxs)])
    ]
    for load in loads:
        load.start()

    loads[0].wait()
    loads[1].wait()
    slot7 = near_ref[7:8, :]
    count = count_ref[...]
    i = lax.broadcasted_iota(jnp.int32, (1, CTR), 1)
    rem15 = i - 15 * ((i * 34953) >> 19)
    shift = (((slot7 >> 13) - q) & 15) - 1 - rem15
    shift = jnp.where(shift < 0, shift + 15, shift)
    full = count == 8
    r = jnp.clip(jnp.max(jnp.where(full, shift, 0)), 0, 14)
    below = jnp.where(full, ZERO_ROW - MARGIN - (slot7 & (PAN - 1)), 0)
    turn = rem15 + r
    turn = jnp.where(turn >= RING, turn - RING, turn)
    mine = turn == lax.broadcasted_iota(jnp.int32, (16, CTR), 0)
    high = jnp.where(mine, (below >> 7).astype(F32), 0.0)
    low = jnp.where(mine, (below & 127).astype(F32), 0.0)
    place = lax.broadcasted_iota(jnp.int32, (REQ, CTR), 0) == ((i * 34953) >> 19)
    lists = lax.dot_general(
        jnp.concatenate([high, low], axis=0).astype(BF16), place.astype(F32).astype(BF16),
        (((1,), (1,)), ((), ())), preferred_element_type=F32).astype(jnp.int32)
    lists = jnp.clip(ZERO_ROW - (lists[0:16] * 128 + lists[16:32]), 0, ZERO_ROW)
    for o in range(1, N_CTR):
        req_v[o - 1] = lists[o - 1:o]
    slot = lax.broadcasted_iota(jnp.int32, (8, CTR), 0)
    idx_v[...] = jnp.where(slot < count, (near_ref[...] - q * PAN + MARGIN) & (N_CTR * PAN - 1), ZERO_ROW)
    to_smem = [pltpu.make_async_copy(idx_v.at[j], idx_s.at[pl.ds(j * CTR, CTR)], smem_sems.at[RING + j]) for j in range(7)]
    for copy in to_smem:
        copy.start()

    pl.semaphore_wait(barrier, RING + 2)

    def request(o):
        return pltpu.make_async_remote_copy(
            req_v.at[o - 1], reqs_v.at[o - 1], req_send.at[o - 1], req_recv.at[o - 1],
            device_id=on_ctr(lax.rem(q + o, N_CTR)), device_id_type=MESH)

    for o in FAR_ORDER:
        request(o).start()

    margins = []
    for k, (buffer, step, start) in enumerate(((prevb, 1, PAN - MARGIN), (nextb, RING, 0))):
        half = pl.ds(pl.multiple_of(core * HALF, HALF), HALF)
        fetch = pltpu.make_async_remote_copy(
            pan_hbm.at[pl.ds(pl.multiple_of(start + core * HALF, HALF), HALF), :], buffer.at[half, :],
            margin_send.at[k], margin_recv.at[k], device_id=on_ctr(lax.rem(q + step, N_CTR)), device_id_type=MESH)
        share = pltpu.make_async_remote_copy(
            buffer.at[half, :], buffer.at[half, :], share_send.at[k], share_recv.at[k],
            device_id=(sibling, q), device_id_type=MESH)
        margins.append((fetch, share))
    for fetch, _ in margins:
        fetch.start()

    box_copy = pltpu.make_async_remote_copy(
        boxs, boxn, box_sems.at[0], box_sems.at[1],
        device_id=(lax.rem(b + N_BOX - 1, N_BOX), q), device_id_type=MESH)
    loads[9].wait()
    box_copy.start()
    tab[pl.ds(ZERO_ROW, 8), :] = jnp.zeros((8, SRC), F32)
    loads[2].wait()

    def widen(k, _):
        rows = pl.ds(pl.multiple_of(k * 512, 512), 512)
        tab[pl.ds(pl.multiple_of(MARGIN + k * 512, 512), 512), :] = loc[rows, :].astype(F32)
        return 0

    lax.fori_loop(0, PAN // 512, widen, 0)
    loads[3].wait()
    loads[4].wait()
    fill(tscaled, xy_ref, rho_ref)
    loads[5].wait()
    loads[6].wait()
    row = lax.broadcasted_iota(jnp.int32, (KP, COEF), 0)
    col = lax.broadcasted_iota(jnp.int32, (KP, COEF), 1)
    source = jnp.where(row < 272, (row & 15) * DEG + (row >> 4), 16 * DEG + row - 272)
    order = (col == source).astype(F32).astype(BF16)
    l2[...] = jnp.dot(order, l2l_ref[...], preferred_element_type=F32).astype(BF16)
    p2[...] = jnp.dot(order, p2l_ref[...], preferred_element_type=F32).astype(BF16)

    def list_copy(o):
        return pltpu.make_async_copy(reqs_v.at[o - 1, 0], req_s.at[pl.ds((o - 1) * REQ, REQ)], smem_sems.at[o - 1])

    def take_request(o, _):
        request(o).wait_recv()
        list_copy(o).start()
        return 0

    lax.fori_loop(1, N_CTR, take_request, 0)

    def have_request(o, _):
        list_copy(o).wait()
        return 0

    lax.fori_loop(1, N_CTR, have_request, 0)

    def answer(o):
        return pltpu.make_async_remote_copy(
            send_v.at[o - 1], far.at[o - 1], far_send.at[o - 1], far_recv.at[o - 1],
            device_id=on_ctr(lax.rem(q + N_CTR - o, N_CTR)), device_id_type=MESH)

    def serve(k, _):
        o = 4 * lax.rem(k // 3 + 1, 4) + 1 + lax.rem(k, 3)
        serve_one(o)
        return 0

    def serve_column(k, _):
        serve_one(4 * k)
        return 0

    def serve_one(o):
        base = (o - 1) * REQ
        mine = req_s.at[pl.ds(base, FAR_USED)]
        for k in range(FAR_USED):
            stage[pl.ds(k, 1), :] = tab[pl.ds(mine[k], 1), :]
        send_v[o - 1] = stage[...].astype(BF16)

    stage[pl.ds(FAR - 8, 8), :] = jnp.zeros((8, SRC), F32)
    lax.fori_loop(0, 12, serve, 0)
    lax.fori_loop(1, 4, serve_column, 0)

    for o in FAR_ORDER[:FIRST]:
        answer(o).start()

    loads[7].wait()
    loads[8].wait()
    box_copy.wait_recv()

    def box_steps(k):
        lanes = pl.ds(pl.multiple_of(k * BLOCK, BLOCK), BLOCK)
        offset = cbox_ref[:, lanes] - b * BOXES
        width = BOXES // PICKS
        picked = None
        for n in range(PICKS):
            ids = lax.broadcasted_iota(jnp.int32, (width, BLOCK), 0) + n * width
            term = jnp.dot(boxv[:, n * width:n * width + width], (ids == offset).astype(F32).astype(BF16), preferred_element_type=F32)
            picked = term if picked is None else picked + term
            yield
        ids = lax.broadcasted_iota(jnp.int32, (128, BLOCK), 0) + BOXES
        picked += jnp.dot(boxn[...], (ids == offset).astype(F32).astype(BF16), preferred_element_type=F32)
        yield
        moved = jnp.dot(l2[...], picked.astype(BF16), preferred_element_type=F32)
        yield
        for h in range(BLOCK // 128):
            cols = pl.ds(pl.multiple_of(k * BLOCK + 128 * h, 128), 128)
            for t in range(4):
                potb[t:t + 1, cols] = evaluate_one(moved[:, 128 * h:128 * h + 128], tscaled, k * (BLOCK // 128) + h, t)
                yield

    def box_only(k, _):
        for _ in box_steps(k):
            pass
        return 0

    lax.fori_loop(0, AHEAD, box_only, 0)
    for fetch, share in margins:
        fetch.wait_recv()
        share.start()
    for o in FAR_ORDER[FIRST:]:
        answer(o).start()
    lax.fori_loop(AHEAD, BLOCKS // 2, box_only, 0)

    for _, share in margins:
        share.wait_recv()

    def widen_margin(k, _):
        rows = pl.ds(pl.multiple_of(k * 512, 512), 512)
        tab[rows, :] = prevb[rows, :].astype(F32)
        tab[pl.ds(pl.multiple_of(MARGIN + PAN + k * 512, 512), 512), :] = nextb[rows, :].astype(F32)
        return 0

    lax.fori_loop(0, MARGIN // 512, widen_margin, 0)
    for copy in to_smem:
        copy.wait()

    def tail_steps(k):
        near_round = acc[pl.ds(pl.multiple_of(k * BLOCK, BLOCK), BLOCK), :].astype(BF16)
        direct = lax.dot_general(p2[...], near_round, (((1,), (1,)), ((), ())), preferred_element_type=F32)
        yield
        for h in range(BLOCK // 128):
            cols = pl.ds(pl.multiple_of(k * BLOCK + 128 * h, 128), 128)
            for t in range(4):
                part = evaluate_one(direct[:, 128 * h:128 * h + 128], tplain, k * (BLOCK // 128) + h, t)
                out_ref[t:t + 1, cols] = potb[t:t + 1, cols] + part
                yield

    def gather(k, add, steps):
        c0 = k * BLOCK
        lists = [idx_s.at[pl.ds(j * CTR + c0, BLOCK)] for j in range(7)]
        for u in range(BLOCK):
            if u % SPACING == 0:
                next(steps, None)
            rows = [tab[pl.ds(lists[j][u], 1), :] for j in range(7)]
            if add:
                rows.append(acc[pl.ds(c0 + u, 1), :])
            while len(rows) > 1:
                rows = [x + y for x, y in zip(rows[::2], rows[1::2])] + ([rows[-1]] if len(rows) % 2 else [])
            acc[pl.ds(c0 + u, 1), :] = rows[0]
        for _ in steps:
            pass

    def plain_steps(k):
        tiles = CTR // 128 // (BLOCKS // 2)
        for n in range(tiles):
            fill_tile(tplain, xy_ref, None, k * tiles + n)
            yield

    def early(k, _):
        gather(k, False, itertools.chain(box_steps(k + BLOCKS // 2), plain_steps(k)))
        return 0

    def late(k, _):
        gather(k, True, itertools.chain(tail_steps(k - BLOCKS // 2), tail_steps(k - 1)))
        return 0

    lax.fori_loop(0, BLOCKS // 2, early, 0)

    def take_far(o, _):
        answer(o).wait_recv()
        return 0

    lax.fori_loop(1, N_CTR, take_far, 0)
    acc[pl.ds(CTR // 2, RING * FAR - CTR // 2), :] = jnp.zeros((RING * FAR - CTR // 2, SRC), F32)
    for m in range(RING):
        rows = far[lax.rem(m + r, RING)].astype(F32)
        at = pl.ds(m, FAR, stride=RING)
        acc[at, :] = acc[at, :] + rows
    lax.fori_loop(BLOCKS // 2, BLOCKS, late, 0)
    for _ in tail_steps(BLOCKS - 1):
        pass

    box_copy.wait_send()
    for group in margins:
        for copy in group:
            copy.wait_send()

    def finish(o, _):
        request(o).wait_send()
        answer(o).wait_send()
        return 0

    lax.fori_loop(1, N_CTR, finish, 0)


def shards(box_locals, centre_box, centre_rho, panel_sources, centre_near, near_count, l2l_op, p2l_op, target_coords):
    vmem = pl.BlockSpec(memory_space=pltpu.VMEM)
    anywhere = pl.BlockSpec(memory_space=pl.ANY)
    dma = pltpu.SemaphoreType.DMA
    return pl.pallas_call(
        kernel,
        out_shape=jax.ShapeDtypeStruct((4, CTR), F32),
        in_specs=[anywhere] * 9,
        out_specs=vmem,
        scratch_shapes=[
            pltpu.VMEM((COEF, BOXES), BF16),
            pltpu.VMEM((1, CTR), jnp.int32),
            pltpu.VMEM((1, CTR), F32),
            pltpu.VMEM((PAN, SRC), BF16),
            pltpu.VMEM((8, CTR), jnp.int32),
            pltpu.VMEM((1, CTR), jnp.int32),
            pltpu.VMEM((COEF, COEF), BF16),
            pltpu.VMEM((COEF, SRC), BF16),
            pltpu.VMEM((2, 4, CTR), F32),
            pltpu.VMEM((COEF, 128), BF16),
            pltpu.VMEM((COEF, 128), BF16),
            pltpu.VMEM((MARGIN, SRC), BF16),
            pltpu.VMEM((MARGIN, SRC), BF16),
            pltpu.VMEM((TAB, SRC), F32),
            pltpu.VMEM((8, CTR), jnp.int32),
            pltpu.VMEM((RING, 1, REQ), jnp.int32),
            pltpu.VMEM((RING, 1, REQ), jnp.int32),
            pltpu.VMEM((FAR, SRC), F32),
            pltpu.VMEM((RING, FAR, SRC), BF16),
            pltpu.VMEM((RING, FAR, SRC), BF16),
            pltpu.VMEM((RING * FAR, SRC), F32),
            pltpu.VMEM((CTR // 128, 192, 128), F32),
            pltpu.VMEM((CTR // 128, 192, 128), F32),
            pltpu.VMEM((KP, COEF), BF16),
            pltpu.VMEM((KP, SRC), BF16),
            pltpu.VMEM((4, CTR), F32),
            pltpu.SMEM((7 * CTR,), jnp.int32),
            pltpu.SMEM((RING * REQ,), jnp.int32),
            dma((10,)), dma((2,)), dma((2,)), dma((2,)), dma((2,)), dma((2,)),
            dma((RING,)), dma((RING,)), dma((RING,)), dma((RING,)), dma((RING + 7,)),
        ],
        compiler_params=pltpu.CompilerParams(collective_id=0, has_side_effects=True, vmem_limit_bytes=60 * 2**20),
        name="qbx",
    )(
        box_locals, centre_box.reshape(1, CTR), centre_rho.reshape(1, CTR), panel_sources, centre_near,
        near_count.reshape(1, CTR), l2l_op, p2l_op, target_coords,
    )


def solution(mesh):
    in_specs = (
        P(None, "box"),
        P(("box", "ctr")),
        P(("box", "ctr")),
        P("ctr", None),
        P(None, ("box", "ctr")),
        P(("box", "ctr")),
        P(),
        P(),
        P(None, None, ("box", "ctr")),
    )
    out_specs = P(None, ("box", "ctr"))
    return jax.shard_map(shards, mesh=mesh, in_specs=in_specs, out_specs=out_specs, check_vma=False)
```

```python
import itertools

import functools

import jax
import jax.numpy as jnp
from jax import lax
from jax.experimental import pallas as pl
from jax.experimental.pallas import tpu as pltpu
from jax.sharding import PartitionSpec as P

N_CTR = 16
N_BOX = 8
CTR = 2048
PAN = 8192
MARGIN = 2048
COEF = 289
DEG = 17
SRC = 128
BOXES = 2048
KP = 296
ZERO_ROW = PAN + 2 * MARGIN
TAB = ZERO_ROW + 8
RING = N_CTR - 1
REQ = 256
FAR = 144
FAR_USED = 137
HALF = MARGIN // 2
FAR_ORDER = (5, 6, 7, 9, 10, 11, 13, 14, 15, 1, 2, 3, 4, 8, 12)
BLOCK = 256
BLOCKS = CTR // BLOCK
PICKS = 4
AHEAD = 1
FIRST = 8
SPACING = 14
MESH = pl.DeviceIdType.MESH
F32 = jnp.float32
BF16 = jnp.bfloat16


def evaluate(grid, table, tile):
    return jnp.concatenate([evaluate_one(grid, table, tile, t) for t in range(4)], axis=0)


def evaluate_one(grid, table, tile, t):
    acc = None
    for b in range(DEG):
        term = grid[16 * b:16 * b + 16, :] * table[tile, pl.ds(8 * b + 4 + t, 1), :]
        acc = term if acc is None else acc + term
    acc = acc * table[tile, pl.ds(t, 16, stride=8), :]
    last = grid[272:296, :] * table[tile, pl.ds(4 + t, 24, stride=8), :]
    last = last * table[tile, pl.ds(8 * 16 + t, 1), :]
    total = (acc[0:8] + acc[8:16]) + (last[0:8] + last[8:16] + last[16:24])
    return jnp.sum(total, axis=0, keepdims=True)


def fill(table, xy, rho_ref):
    def one(tile, _):
        fill_tile(table, xy, rho_ref, tile)
        return 0

    lax.fori_loop(0, CTR // 128, one, 0)


def fill_tile(table, xy, rho_ref, tile):
    lanes = pl.ds(pl.multiple_of(tile * 128, 128), 128)
    x = jnp.concatenate([xy[0, :, lanes], xy[1, :, lanes]], axis=0)
    square = None
    if rho_ref is not None:
        rho = rho_ref[:, lanes]
        x, square = x * rho, rho * rho
    before, now = jnp.ones_like(x), x
    table[tile, pl.ds(0, 8), :] = before
    table[tile, pl.ds(8, 8), :] = now
    for n in range(2, DEG):
        later = 2.0 * x * now - (before if square is None else square * before)
        table[tile, pl.ds(8 * n, 8), :] = later
        before, now = now, later
    table[tile, pl.ds(8 * DEG, 56), :] = jnp.zeros((56, 128), F32)


def kernel(
    box_hbm, cbox_hbm, rho_hbm, pan_hbm, near_hbm, count_hbm, l2l_hbm, p2l_hbm, xy_hbm,
    out_ref,
    boxv, cbox_ref, rho_ref, loc, near_ref, count_ref, l2l_ref, p2l_ref, xy_ref,
    boxs, boxn, prevb, nextb, tab, idx_v, req_v, reqs_v, stage, send_v, far, acc, tplain, tscaled, l2, p2, potb,
    idx_s, req_s,
    load_sems, margin_send, margin_recv, share_send, share_recv, box_sems, req_send, req_recv, far_send, far_recv, smem_sems,
):
    b, q = lax.axis_index("box"), lax.axis_index("ctr")
    core = lax.rem(b, 2)
    sibling = b + 1 - 2 * core

    def on_ctr(other):
        return (b, other)

    barrier = pltpu.get_barrier_semaphore()


    def greet(o, _):
        pl.semaphore_signal(barrier, inc=1, device_id=on_ctr(lax.rem(q + o, N_CTR)), device_id_type=MESH)
        return 0

    lax.fori_loop(1, N_CTR, greet, 0)
    for step in (1, N_BOX - 1):
        pl.semaphore_signal(barrier, inc=1, device_id=(lax.rem(b + step, N_BOX), q), device_id_type=MESH)

    loads = [
        pltpu.make_async_copy(source, target, load_sems.at[k])
        for k, (source, target) in enumerate([
            (near_hbm, near_ref), (count_hbm, count_ref), (pan_hbm, loc), (xy_hbm, xy_ref), (rho_hbm, rho_ref),
            (l2l_hbm, l2l_ref), (p2l_hbm, p2l_ref), (cbox_hbm, cbox_ref), (box_hbm, boxv),
            (box_hbm.at[:, pl.ds(0, 128)], boxs)])
    ]
    for load in loads:
        load.start()

    loads[0].wait()
    loads[1].wait()
    slot7 = near_ref[7:8, :]
    count = count_ref[...]
    i = lax.broadcasted_iota(jnp.int32, (1, CTR), 1)
    rem15 = i - 15 * ((i * 34953) >> 19)
    shift = (((slot7 >> 13) - q) & 15) - 1 - rem15
    shift = jnp.where(shift < 0, shift + 15, shift)
    full = count == 8
    r = jnp.clip(jnp.max(jnp.where(full, shift, 0)), 0, 14)
    below = jnp.where(full, ZERO_ROW - MARGIN - (slot7 & (PAN - 1)), 0)
    turn = rem15 + r
    turn = jnp.where(turn >= RING, turn - RING, turn)
    mine = turn == lax.broadcasted_iota(jnp.int32, (16, CTR), 0)
    high = jnp.where(mine, (below >> 7).astype(F32), 0.0)
    low = jnp.where(mine, (below & 127).astype(F32), 0.0)
    place = lax.broadcasted_iota(jnp.int32, (REQ, CTR), 0) == ((i * 34953) >> 19)
    lists = lax.dot_general(
        jnp.concatenate([high, low], axis=0).astype(BF16), place.astype(F32).astype(BF16),
        (((1,), (1,)), ((), ())), preferred_element_type=F32).astype(jnp.int32)
    lists = jnp.clip(ZERO_ROW - (lists[0:16] * 128 + lists[16:32]), 0, ZERO_ROW)
    for o in range(1, N_CTR):
        req_v[o - 1] = lists[o - 1:o]
    slot = lax.broadcasted_iota(jnp.int32, (8, CTR), 0)
    idx_v[...] = jnp.where(slot < count, (near_ref[...] - q * PAN + MARGIN) & (N_CTR * PAN - 1), ZERO_ROW)
    to_smem = [pltpu.make_async_copy(idx_v.at[j], idx_s.at[pl.ds(j * CTR, CTR)], smem_sems.at[RING + j]) for j in range(7)]
    for copy in to_smem:
        copy.start()

    pl.semaphore_wait(barrier, RING + 2)

    def request(o):
        return pltpu.make_async_remote_copy(
            req_v.at[o - 1], reqs_v.at[o - 1], req_send.at[o - 1], req_recv.at[o - 1],
            device_id=on_ctr(lax.rem(q + o, N_CTR)), device_id_type=MESH)

    for o in FAR_ORDER:
        request(o).start()

    margins = []
    for k, (buffer, step, start) in enumerate(((prevb, 1, PAN - MARGIN), (nextb, RING, 0))):
        half = pl.ds(pl.multiple_of(core * HALF, HALF), HALF)
        fetch = pltpu.make_async_remote_copy(
            pan_hbm.at[pl.ds(pl.multiple_of(start + core * HALF, HALF), HALF), :], buffer.at[half, :],
            margin_send.at[k], margin_recv.at[k], device_id=on_ctr(lax.rem(q + step, N_CTR)), device_id_type=MESH)
        share = pltpu.make_async_remote_copy(
            buffer.at[half, :], buffer.at[half, :], share_send.at[k], share_recv.at[k],
            device_id=(sibling, q), device_id_type=MESH)
        margins.append((fetch, share))
    for fetch, _ in margins:
        fetch.start()

    box_copy = pltpu.make_async_remote_copy(
        boxs, boxn, box_sems.at[0], box_sems.at[1],
        device_id=(lax.rem(b + N_BOX - 1, N_BOX), q), device_id_type=MESH)
    loads[9].wait()
    box_copy.start()
    tab[pl.ds(ZERO_ROW, 8), :] = jnp.zeros((8, SRC), F32)
    loads[2].wait()

    def widen(k, _):
        rows = pl.ds(pl.multiple_of(k * 512, 512), 512)
        tab[pl.ds(pl.multiple_of(MARGIN + k * 512, 512), 512), :] = loc[rows, :].astype(F32)
        return 0

    lax.fori_loop(0, PAN // 512, widen, 0)
    loads[3].wait()
    loads[4].wait()
    fill(tscaled, xy_ref, rho_ref)
    loads[5].wait()
    loads[6].wait()
    row = lax.broadcasted_iota(jnp.int32, (KP, COEF), 0)
    col = lax.broadcasted_iota(jnp.int32, (KP, COEF), 1)
    source = jnp.where(row < 272, (row & 15) * DEG + (row >> 4), 16 * DEG + row - 272)
    order = (col == source).astype(F32).astype(BF16)
    l2[...] = jnp.dot(order, l2l_ref[...], preferred_element_type=F32).astype(BF16)
    p2[...] = jnp.dot(order, p2l_ref[...], preferred_element_type=F32).astype(BF16)

    def list_copy(o):
        return pltpu.make_async_copy(reqs_v.at[o - 1, 0], req_s.at[pl.ds((o - 1) * REQ, REQ)], smem_sems.at[o - 1])

    def take_request(o, _):
        request(o).wait_recv()
        list_copy(o).start()
        return 0

    lax.fori_loop(1, N_CTR, take_request, 0)

    def have_request(o, _):
        list_copy(o).wait()
        return 0

    lax.fori_loop(1, N_CTR, have_request, 0)

    def answer(o):
        return pltpu.make_async_remote_copy(
            send_v.at[o - 1], far.at[o - 1], far_send.at[o - 1], far_recv.at[o - 1],
            device_id=on_ctr(lax.rem(q + N_CTR - o, N_CTR)), device_id_type=MESH)

    def serve(k, _):
        o = 4 * lax.rem(k // 3 + 1, 4) + 1 + lax.rem(k, 3)
        serve_one(o)
        return 0

    def serve_column(k, _):
        serve_one(4 * k)
        return 0

    def serve_one(o):
        base = (o - 1) * REQ
        mine = req_s.at[pl.ds(base, FAR_USED)]
        for k in range(FAR_USED):
            stage[pl.ds(k, 1), :] = tab[pl.ds(mine[k], 1), :]
        send_v[o - 1] = stage[...].astype(BF16)

    stage[pl.ds(FAR - 8, 8), :] = jnp.zeros((8, SRC), F32)
    lax.fori_loop(0, 12, serve, 0)
    lax.fori_loop(1, 4, serve_column, 0)

    for o in FAR_ORDER[:FIRST]:
        answer(o).start()

    loads[7].wait()
    loads[8].wait()
    box_copy.wait_recv()

    def box_steps(k):
        lanes = pl.ds(pl.multiple_of(k * BLOCK, BLOCK), BLOCK)
        offset = cbox_ref[:, lanes] - b * BOXES
        width = BOXES // PICKS
        picked = None
        for n in range(PICKS):
            ids = lax.broadcasted_iota(jnp.int32, (width, BLOCK), 0) + n * width
            term = jnp.dot(boxv[:, n * width:n * width + width], (ids == offset).astype(F32).astype(BF16), preferred_element_type=F32)
            picked = term if picked is None else picked + term
            yield
        ids = lax.broadcasted_iota(jnp.int32, (128, BLOCK), 0) + BOXES
        picked += jnp.dot(boxn[...], (ids == offset).astype(F32).astype(BF16), preferred_element_type=F32)
        yield
        moved = jnp.dot(l2[...], picked.astype(BF16), preferred_element_type=F32)
        yield
        for h in range(BLOCK // 128):
            cols = pl.ds(pl.multiple_of(k * BLOCK + 128 * h, 128), 128)
            for t in range(4):
                potb[t:t + 1, cols] = evaluate_one(moved[:, 128 * h:128 * h + 128], tscaled, k * (BLOCK // 128) + h, t)
                yield

    def box_only(k, _):
        for _ in box_steps(k):
            pass
        return 0

    lax.fori_loop(0, AHEAD, box_only, 0)
    for fetch, share in margins:
        fetch.wait_recv()
        share.start()
    for o in FAR_ORDER[FIRST:]:
        answer(o).start()
    lax.fori_loop(AHEAD, BLOCKS // 2, box_only, 0)

    for _, share in margins:
        share.wait_recv()

    def widen_margin(k, _):
        rows = pl.ds(pl.multiple_of(k * 512, 512), 512)
        tab[rows, :] = prevb[rows, :].astype(F32)
        tab[pl.ds(pl.multiple_of(MARGIN + PAN + k * 512, 512), 512), :] = nextb[rows, :].astype(F32)
        return 0

    lax.fori_loop(0, MARGIN // 512, widen_margin, 0)
    for copy in to_smem:
        copy.wait()

    def tail_steps(k):
        near_round = acc[pl.ds(pl.multiple_of(k * BLOCK, BLOCK), BLOCK), :].astype(BF16)
        direct = lax.dot_general(p2[...], near_round, (((1,), (1,)), ((), ())), preferred_element_type=F32)
        yield
        for h in range(BLOCK // 128):
            cols = pl.ds(pl.multiple_of(k * BLOCK + 128 * h, 128), 128)
            for t in range(4):
                part = evaluate_one(direct[:, 128 * h:128 * h + 128], tplain, k * (BLOCK // 128) + h, t)
                out_ref[t:t + 1, cols] = potb[t:t + 1, cols] + part
                yield

    def gather(k, add, steps):
        c0 = k * BLOCK
        lists = [idx_s.at[pl.ds(j * CTR + c0, BLOCK)] for j in range(7)]
        for u in range(BLOCK):
            if u % SPACING == 0:
                next(steps, None)
            rows = [tab[pl.ds(lists[j][u], 1), :] for j in range(7)]
            if add:
                rows.append(acc[pl.ds(c0 + u, 1), :])
            while len(rows) > 1:
                rows = [x + y for x, y in zip(rows[::2], rows[1::2])] + ([rows[-1]] if len(rows) % 2 else [])
            acc[pl.ds(c0 + u, 1), :] = rows[0]
        for _ in steps:
            pass

    def plain_steps(k):
        tiles = CTR // 128 // (BLOCKS // 2)
        for n in range(tiles):
            fill_tile(tplain, xy_ref, None, k * tiles + n)
            yield

    def early(k, _):
        gather(k, False, itertools.chain(box_steps(k + BLOCKS // 2), plain_steps(k)))
        return 0

    def late(k, _):
        gather(k, True, itertools.chain(tail_steps(k - BLOCKS // 2), tail_steps(k - 1)))
        return 0

    lax.fori_loop(0, BLOCKS // 2, early, 0)

    def take_far(o, _):
        answer(o).wait_recv()
        return 0

    lax.fori_loop(1, N_CTR, take_far, 0)
    acc[pl.ds(CTR // 2, RING * FAR - CTR // 2), :] = jnp.zeros((RING * FAR - CTR // 2, SRC), F32)
    for m in range(RING):
        rows = far[lax.rem(m + r, RING)].astype(F32)
        at = pl.ds(m, FAR, stride=RING)
        acc[at, :] = acc[at, :] + rows
    lax.fori_loop(BLOCKS // 2, BLOCKS, late, 0)
    for _ in tail_steps(BLOCKS - 1):
        pass

    box_copy.wait_send()
    for group in margins:
        for copy in group:
            copy.wait_send()

    def finish(o, _):
        request(o).wait_send()
        answer(o).wait_send()
        return 0

    lax.fori_loop(1, N_CTR, finish, 0)


def shards(box_locals, centre_box, centre_rho, panel_sources, centre_near, near_count, l2l_op, p2l_op, target_coords):
    vmem = pl.BlockSpec(memory_space=pltpu.VMEM)
    anywhere = pl.BlockSpec(memory_space=pl.ANY)
    dma = pltpu.SemaphoreType.DMA
    return pl.pallas_call(
        kernel,
        out_shape=jax.ShapeDtypeStruct((4, CTR), F32),
        in_specs=[anywhere] * 9,
        out_specs=vmem,
        scratch_shapes=[
            pltpu.VMEM((COEF, BOXES), BF16),
            pltpu.VMEM((1, CTR), jnp.int32),
            pltpu.VMEM((1, CTR), F32),
            pltpu.VMEM((PAN, SRC), BF16),
            pltpu.VMEM((8, CTR), jnp.int32),
            pltpu.VMEM((1, CTR), jnp.int32),
            pltpu.VMEM((COEF, COEF), BF16),
            pltpu.VMEM((COEF, SRC), BF16),
            pltpu.VMEM((2, 4, CTR), F32),
            pltpu.VMEM((COEF, 128), BF16),
            pltpu.VMEM((COEF, 128), BF16),
            pltpu.VMEM((MARGIN, SRC), BF16),
            pltpu.VMEM((MARGIN, SRC), BF16),
            pltpu.VMEM((TAB, SRC), F32),
            pltpu.VMEM((8, CTR), jnp.int32),
            pltpu.VMEM((RING, 1, REQ), jnp.int32),
            pltpu.VMEM((RING, 1, REQ), jnp.int32),
            pltpu.VMEM((FAR, SRC), F32),
            pltpu.VMEM((RING, FAR, SRC), BF16),
            pltpu.VMEM((RING, FAR, SRC), BF16),
            pltpu.VMEM((RING * FAR, SRC), F32),
            pltpu.VMEM((CTR // 128, 192, 128), F32),
            pltpu.VMEM((CTR // 128, 192, 128), F32),
            pltpu.VMEM((KP, COEF), BF16),
            pltpu.VMEM((KP, SRC), BF16),
            pltpu.VMEM((4, CTR), F32),
            pltpu.SMEM((7 * CTR,), jnp.int32),
            pltpu.SMEM((RING * REQ,), jnp.int32),
            dma((10,)), dma((2,)), dma((2,)), dma((2,)), dma((2,)), dma((2,)),
            dma((RING,)), dma((RING,)), dma((RING,)), dma((RING,)), dma((RING + 7,)),
        ],
        compiler_params=pltpu.CompilerParams(collective_id=0, has_side_effects=True, vmem_limit_bytes=60 * 2**20),
        name="qbx",
    )(
        box_locals, centre_box.reshape(1, CTR), centre_rho.reshape(1, CTR), panel_sources, centre_near,
        near_count.reshape(1, CTR), l2l_op, p2l_op, target_coords,
    )


def solution(mesh):
    in_specs = (
        P(None, "box"),
        P(("box", "ctr")),
        P(("box", "ctr")),
        P("ctr", None),
        P(None, ("box", "ctr")),
        P(("box", "ctr")),
        P(),
        P(),
        P(None, None, ("box", "ctr")),
    )
    out_specs = P(None, ("box", "ctr"))
    return jax.shard_map(shards, mesh=mesh, in_specs=in_specs, out_specs=out_specs, check_vma=False)
```
